128 devices in a mesh: src: 16 (over x, z_lo, core), tgt: 8 (over y, z_hi).
Axes of the slice: x: 4, y: 4, z: 4 (z_hi: 2, z_lo: 2; z = z_hi * 2 + z_lo), core: 2. Of those that a mesh axis runs over, the one named last changes fastest.
Arguments:
- source_points: float32 [16384, 256], P('src'), may hold values from -24 to 24
- target_points: float32 [32768, 256], P(('tgt', 'src')), may hold values from -24 to 24
- target_potential: float32 [32768], P('tgt'), may hold values from -0.5 to 0.5
Outputs:
- source_potential: float32 [16384], P(('src', 'tgt'))
- target_update: float32 [32768], P(('tgt', 'src'))
- transport_map: float32 [16384, 256], P(('src', 'tgt'))
The draws below stay inside these ranges and needn't reach their ends.
All inputs are finite; a program needn't handle non-finite values.
Results may differ from the reference program's by a relative error of at most 0.0029.
Values sent between devices are 32-bit elements; how exact they have to be, the bound alone decides.
No kernel may reach another device: no remote copies, remote signals or barrier semaphores. Data moves between devices by JAX's collectives and lax.ppermute only.
A program may use at most 64 MiB of HBM per device.

```python
import math
import jax
import jax.numpy as jnp
from jax import lax

D = 256
NS = 16384
NT = 32768


def draw_source_points(key, part):
    key = jax.random.fold_in(key, 11)
    values = jnp.clip(jax.random.normal(key, (NS, D), jnp.float32), -6.0, 6.0)
    return values


def draw_target_points(key, part):
    key = jax.random.fold_in(key, 23)
    values = jnp.clip(jax.random.normal(key, (NT, D), jnp.float32), -6.0, 6.0)
    return values


def block_scale(stream_key, extent, cuts, least, high):
    def one(dim, parts):
        draws = jax.random.uniform(jax.random.fold_in(jax.random.fold_in(stream_key, 6), dim), (parts,), jnp.float32, least / len(cuts), high / len(cuts))
        return jnp.repeat(jnp.exp(draws), extent[dim] // parts).reshape((-1,) + (1,) * (len(extent) - dim - 1))

    factor_of = one(*cuts[0])
    for cut in cuts[1:]:
        factor_of = factor_of * one(*cut)
    return factor_of


def scatter_about(rng, shape, scale, most, pieces=(), kind=jnp.bfloat16):
    values = jax.random.normal(rng, shape, jnp.float32) * scale
    if len(pieces) > 0:
        values = block_scale(rng, shape, pieces, -0.22, 0.18) * values
    return jnp.clip(values, min=-most, max=most).astype(kind)


def setup_inputs(seed: int = 0) -> dict:
    key_of = jax.random.split(jax.random.key(seed), 4)
    source_points = draw_source_points(jax.random.fold_in(key_of[3], 71), 0)
    target_points = draw_target_points(jax.random.fold_in(key_of[3], 71), 0)
    target_potential = scatter_about(key_of[2], (NT,), 0.1, 0.5, ((0, 8),), jnp.float32)
    return {"source_points": source_points, "target_points": target_points, "target_potential": target_potential}


epsilon = 0.05
precise = lax.Precision.HIGHEST


def pair_cost(points, others):
    squares = jnp.sum(points * points, axis=1)
    other_squares = jnp.sum(others * others, axis=1)
    products = lax.dot_general(points, others, (((1,), (1,)), ((), ())), precision=precise, preferred_element_type=jnp.float32)
    return (squares[:, None] + other_squares[None, :] - 2.0 * products) / points.shape[1]


def reference(source_points, target_points, target_potential):
    block_rows = math.gcd(NS, 1024)
    block_count = NS // block_rows
    blocks = source_points.reshape(block_count, block_rows, D)

    def row_logsum(points):
        scores = (target_potential[None, :] - pair_cost(points, target_points)) / epsilon
        highest = jnp.max(scores, axis=1)
        return highest + jnp.log(jnp.sum(jnp.exp(scores - highest[:, None]), axis=1))

    row_values = lax.map(row_logsum, blocks).reshape(NS)
    source_potential = -epsilon * (row_values - math.log(NT))
    potential_blocks = source_potential.reshape(block_count, block_rows)

    def column_step(running, item):
        points, potential = item
        current_top, current_total = running
        scores = (potential[:, None] - pair_cost(points, target_points)) / epsilon
        highest = jnp.maximum(current_top, jnp.max(scores, axis=0))
        total = current_total * jnp.exp(current_top - highest) + jnp.sum(jnp.exp(scores - highest[None, :]), axis=0)
        return (highest, total), None

    column_start = (jnp.full((NT,), -jnp.inf, jnp.float32), jnp.zeros((NT,), jnp.float32))
    (column_top, column_total), unused = lax.scan(column_step, column_start, (blocks, potential_blocks))
    target_update = -epsilon * (column_top + jnp.log(column_total) - math.log(NS))
    targets_low = target_points.astype(jnp.bfloat16)

    def map_rows(points):
        scores = (target_update[None, :] - pair_cost(points, target_points)) / epsilon
        shift = jnp.max(scores, axis=1)
        weights = jnp.exp(scores - shift[:, None])
        denominator = jnp.sum(weights, axis=1)
        numerator = jnp.dot(weights.astype(jnp.bfloat16), targets_low, preferred_element_type=jnp.float32)
        return numerator / denominator[:, None]

    transport_map = lax.map(map_rows, blocks).reshape(NS, D)
    return source_potential, target_update, transport_map
```

```python
import functools
import math

import jax
import jax.numpy as jnp
from jax import lax
from jax.experimental import pallas as pl
from jax.experimental.pallas import tpu as pltpu
from jax.sharding import PartitionSpec as P

epsilon = 0.05
LOG2E = math.log2(math.e)
VMEM = pltpu.VMEM
LIMIT = 40 * 1024 * 1024


def spec():
    return pl.BlockSpec(memory_space=VMEM)


def params():
    return pltpu.CompilerParams(vmem_limit_bytes=LIMIT)


def split_kernel(scale, x_ref, out_ref):
    x = x_ref[...] * scale
    width = x.shape[1]
    high = x.astype(jnp.bfloat16)
    low = (x - high.astype(jnp.float32)).astype(jnp.bfloat16)
    out_ref[:, 0:width] = high
    out_ref[:, width : 2 * width] = high
    out_ref[:, 2 * width : 3 * width] = low


def transposed(block):
    return block.T


def score_kernel(ids, first, last, block, *refs):
    refs = list(refs)
    x_ref, ta_ref, tb_ref, pot_ref = refs[:4]
    refs = refs[4:]
    if not first:
        top_in, total_in = refs[:2]
        refs = refs[2:]
    score_ref, low_ref, top_ref, total_ref = refs[:4]
    piece, width = ta_ref.shape
    me = lax.axis_index("src")
    factor = LOG2E / epsilon
    parts = []
    offsets = []
    for k, t_ref in enumerate((ta_ref, tb_ref)):
        t = t_ref[...]
        low_ref[k * piece : (k + 1) * piece, :] = t.astype(jnp.bfloat16)
        tt = t.T
        high = tt.astype(jnp.bfloat16)
        low = (tt - high.astype(jnp.float32)).astype(jnp.bfloat16)
        parts.append(jnp.concatenate([high, low, high], axis=0))
        squares = jnp.sum(tt * tt, axis=0, keepdims=True)
        potential = pot_ref[pl.ds(ids[k](me), 1), :]
        offsets.append(potential * factor - squares * (factor / width))
    right = jnp.concatenate(parts, axis=1)
    offset = jnp.concatenate(offsets, axis=1)
    rows = x_ref.shape[0]
    columns = right.shape[1]
    for start in range(0, rows, block):
        at = slice(start, start + block)
        score = jnp.dot(x_ref[at, :], right, preferred_element_type=jnp.float32) + offset
        score_ref[at, :] = score
        tiles = [score[:, k : k + 128] for k in range(0, columns, 128)]
        top = functools.reduce(jnp.maximum, tiles)
        if not first:
            old = top_in[at, :]
            top = jnp.maximum(top, old)
        total = sum(jnp.exp2(tile - top) for tile in tiles)
        if not first:
            total = total + total_in[at, :] * jnp.exp2(old - top)
        top_ref[at, :] = top
        total_ref[at, :] = total
    if last:
        row_ref = refs[4]
        for k in range(rows // 128):
            at = slice(k * 128, (k + 1) * 128)
            top = top_ref[at, :].T
            total = total_ref[at, :].T
            highest = jnp.max(top, axis=0, keepdims=True)
            whole = jnp.sum(total * jnp.exp2(top - highest), axis=0, keepdims=True)
            row_ref[k : k + 1, :] = highest + jnp.log2(whole)


def column_kernel(groups, log_targets, *refs):
    score_refs = refs[: len(groups)]
    rows_ref, column_ref, level_ref, add_ref = refs[len(groups) :]
    parts = [rows_ref[k] for k in range(rows_ref.shape[0])]
    highest = functools.reduce(jnp.maximum, parts)
    level = highest + jnp.log2(sum(jnp.exp2(part - highest) for part in parts))
    level_ref[...] = level
    add = log_targets - level
    for k in range(add.shape[0]):
        add_ref[k * 128 : (k + 1) * 128, :] = jnp.broadcast_to(add[k : k + 1, :], (128, 128)).T
    me = lax.axis_index("src")
    rows = add_ref.shape[0]
    step = 128
    for group, score_ref in zip(groups, score_refs, strict=True):
        piece = score_ref.shape[1] // 2
        for k in range(2):
            outs = []
            for c in range(k * piece, (k + 1) * piece, 128):
                top = None
                for r in range(0, rows, step):
                    v = score_ref[r : r + step, c : c + 128] + add_ref[r : r + step, :]
                    v = jnp.max(v.reshape(step // 8, 8, 128), axis=0)
                    top = v if top is None else jnp.maximum(top, v)
                high = jnp.max(top, axis=0, keepdims=True)
                total = None
                for r in range(0, rows, step):
                    v = score_ref[r : r + step, c : c + 128] + add_ref[r : r + step, :]
                    v = jnp.sum(jnp.exp2(v - high).reshape(step // 8, 8, 128), axis=0)
                    total = v if total is None else total + v
                outs.append(high + jnp.log2(jnp.sum(total, axis=0, keepdims=True)))
            column_ref[pl.ds(group[k](me), 1), :] = jnp.concatenate(outs, axis=1)


def map_kernel(groups, block, *refs):
    count = len(groups)
    score_refs = refs[:count]
    low_refs = refs[count : 2 * count]
    add_ref, parts_ref, out_ref, level_ref, sum_ref, weight_ref = refs[2 * count :]
    parts = [parts_ref[k] for k in range(parts_ref.shape[0])]
    highest = functools.reduce(jnp.maximum, parts)
    level_ref[...] = highest + jnp.log2(sum(jnp.exp2(part - highest) for part in parts))
    me = lax.axis_index("src")
    rows = add_ref.shape[0]
    for g, group in enumerate(groups):
        level = jnp.concatenate([level_ref[pl.ds(group[k](me), 1), :] for k in range(2)], axis=1)
        columns = level.shape[1]
        for start in range(0, rows, block):
            at = slice(start, start + block)
            add = add_ref[at, :]
            total = None
            weights = []
            for c in range(0, columns, 128):
                w = jnp.exp2(score_refs[g][at, c : c + 128] + add - level[:, c : c + 128])
                total = w if total is None else total + w
                weights.append(w.astype(jnp.bfloat16))
            part = jnp.dot(
                jnp.concatenate(weights, axis=1), low_refs[g][...], preferred_element_type=jnp.float32
            )
            for r in range(0, block, 128):
                k = (start + r) // 128
                if g == 0:
                    out_ref[k, 0:128, :] = part[r : r + 128, :]
                else:
                    out_ref[k, 0:128, :] += part[r : r + 128, :]
            if g == 0:
                sum_ref[at, :] = total
            else:
                sum_ref[at, :] += total
    for k in range(rows // 128):
        total = jnp.sum(sum_ref[k * 128 : (k + 1) * 128, :].T, axis=0, keepdims=True)
        out_ref[k, 128:136, :] = jnp.broadcast_to(
            jnp.concatenate([total] * (out_ref.shape[2] // 128), axis=1), (8, out_ref.shape[2])
        )


def quotient_kernel(parts_ref, out_ref):
    rows, width = out_ref.shape
    numerator = parts_ref[0, 0:rows, :]
    denominator = parts_ref[0, rows : rows + 8, 0:128]
    for k in range(1, parts_ref.shape[0]):
        numerator = numerator + parts_ref[k, 0:rows, :]
        denominator = denominator + parts_ref[k, rows : rows + 8, 0:128]
    inverse = jnp.broadcast_to(1.0 / denominator[0:1, :], (128, 128)).T
    for c in range(0, width, 128):
        out_ref[:, c : c + 128] = numerator[:, c : c + 128] * inverse


def shards(source_points, target_points, target_potential):
    sources, tgts = lax.axis_size("src"), lax.axis_size("tgt")
    rows, width = source_points.shape
    columns = target_potential.shape[0]
    piece = target_points.shape[0]
    f32, bf16 = jnp.float32, jnp.bfloat16
    me, mine = lax.axis_index("src"), lax.axis_index("tgt")

    def send(value, to):
        return lax.ppermute(value, "src", [(i, to(i)) for i in range(sources)])

    twin = lambda i: i ^ 1
    across = lambda i: i ^ 2
    far = lambda i: i ^ 8
    ahead = lambda i: (i + 4) % sources
    behind = lambda i: (i + sources - 4) % sources

    own = target_points
    z = send(own, across)
    xp = send(own, ahead)
    xm = send(own, behind)
    x2 = send(own, far)
    zp = send(z, ahead)
    zm = send(z, behind)
    z2 = send(x2, across)
    ident = lambda i: i
    arrivals = [
        (own, ident),
        (xp, behind),
        (xm, ahead),
        (z, across),
        (x2, far),
        (zp, lambda i: across(behind(i))),
        (zm, lambda i: across(ahead(i))),
        (z2, lambda i: across(far(i))),
    ]
    groups = [(of, lambda i, of=of: twin(of(i))) for _, of in arrivals]

    def twin_of(value):
        return send(value, twin)

    left = pl.pallas_call(
        functools.partial(split_kernel, 2.0 * LOG2E / (epsilon * width)),
        out_shape=VMEM((rows, 3 * width), bf16),
        in_specs=[spec()],
        out_specs=spec(),
        compiler_params=params(),
        name="split",
    )(source_points)
    pot = target_potential.reshape(sources, piece)
    state = ()
    scores, lows = [], []
    for g, (block, _) in enumerate(arrivals):
        first, last = g == 0, g == len(arrivals) - 1
        outs = [VMEM((rows, 2 * piece), f32), VMEM((2 * piece, width), bf16), VMEM((rows, 128), f32), VMEM((rows, 128), f32)]
        if last:
            outs.append(VMEM((rows // 128, 128), f32))
        result = pl.pallas_call(
            functools.partial(score_kernel, groups[g], first, last, 256),
            out_shape=outs,
            in_specs=[spec()] * (4 + len(state)),
            out_specs=[spec()] * len(outs),
            input_output_aliases={} if first else {4: 2, 5: 3},
            compiler_params=params(),
            cost_estimate=pl.CostEstimate(
                flops=2 * rows * 2 * piece * 3 * width, bytes_accessed=4 * rows * piece, transcendentals=rows * 2 * piece
            ),
            name="score",
        )(left, block, twin_of(block), pot, *state)
        scores.append(result[0])
        lows.append(result[1])
        state = tuple(result[2:4])
    row_level = result[4]
    spread = jnp.broadcast_to(row_level[None], (tgts,) + row_level.shape)
    row_levels = lax.all_to_all(spread, "tgt", 0, 0)
    column_level, level, add = pl.pallas_call(
        functools.partial(column_kernel, groups, math.log2(columns * tgts)),
        out_shape=[VMEM((sources, piece), f32), VMEM((rows // 128, 128), f32), VMEM((rows, 128), f32)],
        in_specs=[spec()] * (len(scores) + 1),
        out_specs=[spec()] * 3,
        compiler_params=params(),
        name="columns",
    )(*scores, row_levels)
    spread = jnp.broadcast_to(column_level[None], (sources,) + column_level.shape)
    column_levels = lax.all_to_all(spread, "src", 0, 0)
    share = rows // tgts
    partial_map, column_whole = pl.pallas_call(
        functools.partial(map_kernel, groups, 256),
        out_shape=[VMEM((tgts, share + 8, width), f32), VMEM((sources, piece), f32)],
        in_specs=[spec()] * (2 * len(scores) + 2),
        out_specs=[spec()] * 2,
        scratch_shapes=[VMEM((rows, 128), f32), VMEM((8, 128), f32)],
        compiler_params=params(),
        name="map",
    )(*scores, *lows, add, column_levels)
    received = lax.all_to_all(partial_map, "tgt", 0, 0)
    transport_map = pl.pallas_call(
        quotient_kernel,
        out_shape=jax.ShapeDtypeStruct((share, width), f32),
        in_specs=[spec()],
        out_specs=spec(),
        compiler_params=params(),
        name="quotient",
    )(received)
    own_rows = lax.dynamic_slice_in_dim(source_points, mine * share, share, 0)
    squares = jnp.sum(own_rows * own_rows, axis=1) / width
    own_level = lax.dynamic_slice_in_dim(level, mine, 1, 0).reshape(share)
    own_source = squares - epsilon * (own_level / LOG2E - math.log(columns * tgts))
    own_column = lax.dynamic_slice_in_dim(column_whole, me, 1, 0).reshape(piece)
    own_potential = lax.dynamic_slice_in_dim(pot, me, 1, 0).reshape(piece)
    own_target = own_potential - epsilon * (own_column / LOG2E - math.log(rows * sources))
    return own_source, own_target, transport_map


def solution(mesh):
    return jax.shard_map(
        shards,
        mesh=mesh,
        in_specs=(P("src", None), P(("tgt", "src"), None), P("tgt")),
        out_specs=(P(("src", "tgt")), P(("tgt", "src")), P(("src", "tgt"), None)),
        check_vma=False,
    )
```

```python
import functools
import math

import jax
import jax.numpy as jnp
from jax import lax
from jax.experimental import pallas as pl
from jax.experimental.pallas import tpu as pltpu
from jax.sharding import Mesh
from jax.sharding import PartitionSpec as P

epsilon = 0.05
LOG2E = math.log2(math.e)
VMEM = pltpu.VMEM
LIMIT = 18 * 1024 * 1024


def spec():
    return pl.BlockSpec(memory_space=VMEM)


def params():
    return pltpu.CompilerParams(vmem_limit_bytes=LIMIT)


def split_kernel(scale, own, x_ref, out_ref, *square_ref):
    x = x_ref[...]
    width = x.shape[1]
    if own:
        mine = lax.axis_index("y") * lax.axis_size("zh") + lax.axis_index("zh")
        some = x_ref[pl.ds(pl.multiple_of(mine * 128, 128), 128), :]
        square_ref[0][...] = jnp.sum((some * some).T, axis=0, keepdims=True)
    x = x * scale
    high = x.astype(jnp.bfloat16)
    low = (x - high.astype(jnp.float32)).astype(jnp.bfloat16)
    out_ref[:, 0:width] = high
    out_ref[:, width : 2 * width] = high
    out_ref[:, 2 * width : 3 * width] = low


def place(of):
    return lax.rem(lax.axis_index("x") + of[0], lax.axis_size("x"))


def half_of(of):
    half = lax.axis_index("zl")
    return 1 - half if of[1] else half


def piece_of(of):
    return (place(of) * 2 + half_of(of)) * 2 + lax.axis_index("c")


def column_of(of):
    return place(of) * 2 + half_of(of)


def potential_of(pot_ref, of, piece):
    lines = piece // 128
    start = piece_of(of) * lines
    return jnp.concatenate([pot_ref[pl.ds(start + k, 1), :] for k in range(lines)], axis=1)


def score_rows(x_ref, right_ref, offset_ref, old, score_ref, top_ref, total_ref, block):
    rows, columns = score_ref.shape
    for start in range(0, rows, block):
        at = slice(start, start + block)
        score = jnp.dot(x_ref[at, :], right_ref[...], preferred_element_type=jnp.float32)
        score = score + offset_ref[0:1, :]
        score_ref[at, :] = score
        tiles = [score[:, k : k + 128] for k in range(0, columns, 128)]
        top = functools.reduce(jnp.maximum, tiles)
        if old is not None:
            before = old[0][at, :]
            top = jnp.maximum(top, before)
        total = sum(jnp.exp2(tile - top) for tile in tiles)
        if old is not None:
            total = total + old[1][at, :] * jnp.exp2(before - top)
        top_ref[at, :] = top
        total_ref[at, :] = total


def score_kernel(group, first, last, *refs):
    left_refs, t_refs, pot_refs, refs = refs[:2], refs[2:4], refs[4:6], refs[6:]
    old = (None, None)
    if not first:
        old, refs = (refs[0:2], refs[2:4]), refs[4:]
    score_refs, low_ref, state_refs, refs = refs[:2], refs[2], (refs[3:5], refs[5:7]), refs[7:]
    right_ref, offset_ref = refs[-2:]
    piece, width = t_refs[0].shape
    factor = LOG2E / epsilon
    for k, of in enumerate(group):
        at = slice(k * piece, (k + 1) * piece)
        t = t_refs[k][...]
        low_ref[at, :] = t.astype(jnp.bfloat16)
        tt = t.T
        high = tt.astype(jnp.bfloat16)
        low = (tt - high.astype(jnp.float32)).astype(jnp.bfloat16)
        right_ref[0:width, at] = high
        right_ref[width : 2 * width, at] = low
        right_ref[2 * width : 3 * width, at] = high
        squares = jnp.sum(tt * tt, axis=0, keepdims=True)
        potential = potential_of(pot_refs[int(of[1])], of, piece)
        offset_ref[0:1, at] = potential * factor - squares * (factor / width)
    for side in range(2):
        score_rows(left_refs[side], right_ref, offset_ref, old[side], score_refs[side], *state_refs[side], 256)
        if last:
            top_ref, total_ref = state_refs[side]
            for k in range(top_ref.shape[0] // 128):
                at = slice(k * 128, (k + 1) * 128)
                top = top_ref[at, :].T
                total = total_ref[at, :].T
                highest = jnp.max(top, axis=0, keepdims=True)
                whole = jnp.sum(total * jnp.exp2(top - highest), axis=0, keepdims=True)
                refs[0][side, k : k + 1, :] = highest + jnp.log2(whole)


def log_sum(parts):
    highest = functools.reduce(jnp.maximum, parts)
    return highest + jnp.log2(sum(jnp.exp2(part - highest) for part in parts))


def column_kernel(groups, log_targets, width, *refs):
    count = len(groups)
    score_refs = (refs[:count], refs[count : 2 * count])
    rows_ref, square_ref, column_ref, own_ref = refs[2 * count : 2 * count + 4]
    add_refs = refs[2 * count + 4 :]
    half = lax.axis_index("c")
    group = rows_ref.shape[0] // 2
    mine = lax.axis_index("y") * lax.axis_size("zh") + lax.axis_index("zh")
    for side in range(2):
        parts = [rows_ref[half * group + k, side] for k in range(group)]
        parts += [rows_ref[(1 - half) * group + k, 1 - side] for k in range(group)]
        add = log_targets - log_sum(parts)
        for k in range(add.shape[0]):
            add_refs[side][k * 128 : (k + 1) * 128, :] = jnp.broadcast_to(add[k : k + 1, :], (128, 128)).T
        if side == 0:
            chosen = jnp.where(lax.broadcasted_iota(jnp.int32, add.shape, 0) == mine, add, 0.0)
            chosen = jnp.sum(chosen, axis=0, keepdims=True)
            own_ref[...] = square_ref[...] / width + chosen * (epsilon / LOG2E)
    rows = add_refs[0].shape[0]
    step = 64
    columns = score_refs[0][0].shape[1]
    tiles = [(g, slice(c, c + 128)) for g in range(count) for c in range(0, columns, 128)]

    def sweep(side):
        def one(n, sums):
            at = pl.ds(pl.multiple_of(n * step, step), step)
            add = add_refs[side][at, :]
            out = []
            for (g, c), total in zip(tiles, sums, strict=True):
                v = jnp.exp2(score_refs[side][g][at, c] + add)
                out.append(total + jnp.sum(v.reshape(step // 8, 8, 128), axis=0))
            return tuple(out)

        return one

    sums = tuple(jnp.zeros((8, 128), jnp.float32) for _ in tiles)
    for side in range(2):
        sums = lax.fori_loop(0, rows // step, sweep(side), sums)
    sums = [jnp.sum(total, axis=0, keepdims=True) for total in sums]
    least = jnp.min(functools.reduce(jnp.minimum, sums))
    for g, group in enumerate(groups):
        for k, of in enumerate(group):
            n = (g * len(group) + k) * (columns // 128 // len(group))
            some = sums[n : n + columns // 128 // len(group)]
            column_ref[pl.ds(column_of(of), 1), :] = jnp.log2(jnp.concatenate(some, axis=1))

    @pl.when(jnp.logical_not(least > 2.0**-80))
    def _():
        safe_columns(groups, score_refs, add_refs, column_ref)


def safe_columns(groups, score_refs, add_refs, column_ref):
    rows = add_refs[0].shape[0]
    step = 64
    for g, of in enumerate(groups):
        piece = score_refs[0][g].shape[1] // 2
        for k in range(2):
            at = [slice(c, c + 128) for c in range(k * piece, (k + 1) * piece, 128)]
            tops = [None] * len(at)
            for side in range(2):
                for r in range(0, rows, step):
                    add = add_refs[side][r : r + step, :]
                    for n, c in enumerate(at):
                        v = score_refs[side][g][r : r + step, c] + add
                        v = jnp.max(v.reshape(step // 8, 8, 128), axis=0)
                        tops[n] = v if tops[n] is None else jnp.maximum(tops[n], v)
            tops = [jnp.max(top, axis=0, keepdims=True) for top in tops]
            totals = [None] * len(at)
            for side in range(2):
                for r in range(0, rows, step):
                    add = add_refs[side][r : r + step, :]
                    for n, c in enumerate(at):
                        v = jnp.exp2(score_refs[side][g][r : r + step, c] + add - tops[n])
                        v = jnp.sum(v.reshape(step // 8, 8, 128), axis=0)
                        totals[n] = v if totals[n] is None else totals[n] + v
            outs = [top + jnp.log2(jnp.sum(total, axis=0, keepdims=True)) for top, total in zip(tops, totals, strict=True)]
            column_ref[pl.ds(column_of(of[k]), 1), :] = jnp.concatenate(outs, axis=1)


def map_kernel(groups, block, log_sources, *refs):
    count = len(groups)
    score_refs, refs = refs[:count], refs[count:]
    low_refs, refs = refs[:count], refs[count:]
    add_ref, parts_ref, refs = refs[0], refs[1], refs[2:]
    if log_sources is not None:
        pot_ref, out_ref, own_ref, level_ref, sum_ref = refs
    else:
        out_ref, level_ref, sum_ref = refs
    parts = [parts_ref[k] for k in range(parts_ref.shape[0])]
    level_ref[...] = log_sum(parts)
    if log_sources is not None:
        own = level_ref[pl.ds(column_of((0, False)), 1), :]
        own_ref[...] = potential_of(pot_ref, (0, False), own.shape[1]) - epsilon * (own / LOG2E - log_sources)
    rows = add_ref.shape[0]
    for g, group in enumerate(groups):
        level = jnp.concatenate([level_ref[pl.ds(column_of(of), 1), :] for of in group], axis=1)
        columns = level.shape[1]
        for start in range(0, rows, block):
            at = slice(start, start + block)
            add = add_ref[at, :]
            total = None
            weights = []
            for c in range(0, columns, 128):
                w = jnp.exp2(score_refs[g][at, c : c + 128] + add - level[:, c : c + 128])
                total = w if total is None else total + w
                weights.append(w.astype(jnp.bfloat16))
            part = jnp.dot(
                jnp.concatenate(weights, axis=1), low_refs[g][...], preferred_element_type=jnp.float32
            )
            for r in range(0, block, 128):
                k = (start + r) // 128
                if g == 0:
                    out_ref[k, 0:128, :] = part[r : r + 128, :]
                else:
                    out_ref[k, 0:128, :] += part[r : r + 128, :]
            if g == 0:
                sum_ref[at, :] = total
            else:
                sum_ref[at, :] += total
    for k in range(rows // 128):
        total = jnp.sum(sum_ref[k * 128 : (k + 1) * 128, :].T, axis=0, keepdims=True)
        out_ref[k, 128:136, :] = jnp.broadcast_to(
            jnp.concatenate([total] * (out_ref.shape[2] // 128), axis=1), (8, out_ref.shape[2])
        )


def quotient_kernel(parts_ref, out_ref):
    rows, width = out_ref.shape
    numerator = parts_ref[0, 0:rows, :]
    denominator = parts_ref[0, rows : rows + 8, 0:128]
    for k in range(1, parts_ref.shape[0]):
        numerator = numerator + parts_ref[k, 0:rows, :]
        denominator = denominator + parts_ref[k, rows : rows + 8, 0:128]
    inverse = jnp.broadcast_to(1.0 / denominator[0:1, :], (128, 128)).T
    for c in range(0, width, 128):
        out_ref[:, c : c + 128] = numerator[:, c : c + 128] * inverse


def call(kernel, name, outs, *args, scratch=(), aliases=None):
    return pl.pallas_call(
        kernel,
        out_shape=outs,
        in_specs=[spec()] * len(args),
        out_specs=[spec()] * len(outs),
        scratch_shapes=list(scratch),
        input_output_aliases=aliases or {},
        compiler_params=params(),
        name=name,
    )(*args)


def shards(source_points, target_points, target_potential):
    sizes = {name: lax.axis_size(name) for name in ("x", "zl", "c", "y", "zh")}
    across_x = sizes["x"]
    rows, width = source_points.shape
    piece = target_points.shape[0]
    tgts = sizes["y"] * sizes["zh"]
    sources = sizes["x"] * sizes["zl"] * sizes["c"]
    log_targets = math.log2(target_potential.shape[0] * tgts)
    f32, bf16 = jnp.float32, jnp.bfloat16
    share = rows // tgts

    trade = []
    for zl in range(2):
        for c in range(2):
            for zh in range(2):
                trade.append((zl * 4 + c * 2 + zh, (1 - zl) * 4 + c * 2 + (zh ^ c)))

    def traded(value):
        return lax.ppermute(value, ("zl", "c", "zh"), trade)

    def along(value, by):
        return lax.ppermute(value, "x", [(i, (i + by) % across_x) for i in range(across_x)])

    def twin(value):
        return lax.ppermute(value, "c", [(0, 1), (1, 0)])

    def along_ring(by):
        return along(target_points, by)

    other_points = twin(source_points)
    other_pot = traded(target_potential)
    blocks = {(0, False): target_points, (0, True): traded(target_points)}
    for by in (1, 2, 3):
        blocks[(across_x - by, False)] = along_ring(by)
    groups = [
        [(0, False), (0, True)],
        [(1, False), (3, False)],
        [(2, False), (1, True)],
        [(3, True), (2, True)],
    ]
    scale = 2.0 * LOG2E / (epsilon * width)
    left, squares = call(
        functools.partial(split_kernel, scale, True),
        "split",
        [VMEM((rows, 3 * width), bf16), VMEM((1, share), f32)],
        source_points,
    )
    (other_left,) = call(
        functools.partial(split_kernel, scale, False), "split", [VMEM((rows, 3 * width), bf16)], other_points
    )
    pot, other_pot = target_potential.reshape(-1, 128), other_pot.reshape(-1, 128)
    own_scores, other_scores, lows, state = [], [], [], ()
    for g, group in enumerate(groups):
        first, last = g == 0, g == len(groups) - 1
        outs = [VMEM((rows, 2 * piece), f32)] * 2 + [VMEM((2 * piece, width), bf16)] + [VMEM((rows, 128), f32)] * 4
        if last:
            outs.append(VMEM((2, rows // 128, 128), f32))
        result = call(
            functools.partial(score_kernel, group, first, last),
            "score",
            outs,
            left,
            other_left,
            *(blocks[of] for of in group),
            pot,
            other_pot,
            *state,
            scratch=[VMEM((3 * width, 2 * piece), bf16), VMEM((8, 2 * piece), f32)],
            aliases={} if first else {6 + k: 3 + k for k in range(4)},
        )
        own_scores.append(result[0])
        other_scores.append(result[1])
        lows.append(result[2])
        state = tuple(result[3:7])
        if g == 0:
            blocks[(3, False)], blocks[(1, False)], *state = lax.optimization_barrier(
                (blocks[(3, False)], blocks[(1, False)]) + state
            )
            blocks[(1, True)] = traded(blocks[(1, False)])
            blocks[(3, True)] = traded(blocks[(3, False)])
            blocks[(2, True)] = traded(blocks[(2, False)])
        if g == 1:
            pass
    levels = result[7]
    row_axes = ("c", "y", "zh")
    spread = jnp.broadcast_to(levels[None], (2 * tgts,) + levels.shape)
    row_levels = lax.all_to_all(spread, row_axes, 0, 0)
    column_level, own_source, add, other_add = call(
        functools.partial(column_kernel, groups, log_targets, width),
        "columns",
        [VMEM((2 * across_x, piece), f32), VMEM((1, share), f32), VMEM((rows, 128), f32), VMEM((rows, 128), f32)],
        *own_scores,
        *other_scores,
        row_levels,
        squares,
    )
    spread = jnp.broadcast_to(column_level[None], (2 * across_x,) + column_level.shape)
    members = []
    for layer in range(2):
        for c in range(2):
            members.append([((k * 2 + zl) * 2 + c) * 2 + (layer ^ (zl & c)) for k in range(across_x) for zl in range(2)])
    column_levels = lax.all_to_all(spread, ("x", "zl", "c", "zh"), 0, 0, axis_index_groups=members)
    scratch = [VMEM(column_level.shape, f32), VMEM((rows, 128), f32)]
    partial_out = VMEM((tgts, share + 8, width), f32)
    (other_map,) = call(
        functools.partial(map_kernel, groups, 256, None),
        "map_other",
        [partial_out],
        *other_scores,
        *lows,
        other_add,
        column_levels,
        scratch=scratch,
    )
    returned = twin(other_map)
    own_map, own_target = call(
        functools.partial(map_kernel, groups, 256, math.log(rows * sources)),
        "map",
        [partial_out, VMEM((1, piece), f32)],
        *own_scores,
        *lows,
        add,
        column_levels,
        pot,
        scratch=scratch,
    )
    summed, own_source, own_target = lax.optimization_barrier(
        (own_map + returned, own_source.reshape(share), own_target.reshape(piece))
    )
    received = lax.all_to_all(summed, ("y", "zh"), 0, 0)
    transport_map = pl.pallas_call(
        quotient_kernel,
        out_shape=jax.ShapeDtypeStruct((share, width), f32),
        in_specs=[spec()],
        out_specs=spec(),
        compiler_params=params(),
        name="quotient",
    )(received)
    return own_source, own_target, transport_map


def solution(mesh):
    fine = Mesh(mesh.devices.reshape(4, 2, 2, 4, 2), ("x", "zl", "c", "y", "zh"))
    src, tgt = ("x", "zl", "c"), ("y", "zh")
    return jax.shard_map(
        shards,
        mesh=fine,
        in_specs=(P(src, None), P(tgt + src, None), P(tgt)),
        out_specs=(P(src + tgt), P(tgt + src), P(src + tgt, None)),
        check_vma=False,
    )
```

```python
import functools
import math

import jax
import jax.numpy as jnp
from jax import lax
from jax.experimental import pallas as pl
from jax.experimental.pallas import tpu as pltpu
from jax.sharding import Mesh
from jax.sharding import PartitionSpec as P

epsilon = 0.05
LOG2E = math.log2(math.e)
VMEM = pltpu.VMEM
LIMIT = 18 * 1024 * 1024


def spec():
    return pl.BlockSpec(memory_space=VMEM)


def params():
    return pltpu.CompilerParams(vmem_limit_bytes=LIMIT)


def split_kernel(scale, own, x_ref, out_ref, *square_ref):
    x = x_ref[...]
    width = x.shape[1]
    if own:
        mine = lax.axis_index("y") * lax.axis_size("zh") + lax.axis_index("zh")
        some = x_ref[pl.ds(pl.multiple_of(mine * 128, 128), 128), :]
        square_ref[0][...] = jnp.sum((some * some).T, axis=0, keepdims=True)
    x = x * scale
    high = x.astype(jnp.bfloat16)
    low = (x - high.astype(jnp.float32)).astype(jnp.bfloat16)
    out_ref[:, 0:width] = high
    out_ref[:, width : 2 * width] = high
    out_ref[:, 2 * width : 3 * width] = low


def place(of):
    return lax.rem(lax.axis_index("x") + of[0], lax.axis_size("x"))


def half_of(of):
    half = lax.axis_index("zl")
    return 1 - half if of[1] else half


def piece_of(of):
    return (place(of) * 2 + half_of(of)) * 2 + lax.axis_index("c")


def column_of(of):
    return place(of) * 2 + half_of(of)


def potential_of(pot_ref, base, of, piece):
    lines = piece // 128
    start = base + piece_of(of) * lines
    return jnp.concatenate([pot_ref[pl.ds(start + k, 1), :][:, 0:128] for k in range(lines)], axis=1)


def pack_kernel(starts, *refs):
    out_ref = refs[-1]
    for start, ref in zip(starts, refs[-1 - len(starts) : -1], strict=True):
        rows, width = ref.shape
        out_ref[start : start + rows, 0:width] = ref[...]
        if width < out_ref.shape[1]:
            out_ref[start : start + rows, width:] = jnp.zeros((rows, out_ref.shape[1] - width), jnp.float32)


def score_rows(x_ref, right_ref, offset_ref, old, score_ref, top_ref, total_ref, block):
    rows, columns = score_ref.shape
    for start in range(0, rows, block):
        at = slice(start, start + block)
        score = jnp.dot(x_ref[at, :], right_ref[...], preferred_element_type=jnp.float32)
        score = score + offset_ref[0:1, :]
        score_ref[at, :] = score
        tiles = [score[:, k : k + 128] for k in range(0, columns, 128)]
        top = functools.reduce(jnp.maximum, tiles)
        if old is not None:
            before = old[0][at, :]
            top = jnp.maximum(top, before)
        total = sum(jnp.exp2(tile - top) for tile in tiles)
        if old is not None:
            total = total + old[1][at, :] * jnp.exp2(before - top)
        top_ref[at, :] = top
        total_ref[at, :] = total


def score_kernel(group, piece, sources, base, first, last, *refs):
    left_refs, refs = refs[:2], refs[2:]
    block_refs, pot_ref, refs = refs[: len(sources)], refs[len(sources)], refs[len(sources) + 1 :]
    old = (None, None)
    if not first:
        old, refs = (refs[0:2], refs[2:4]), refs[4:]
    score_refs, low_ref, state_refs, refs = refs[:2], refs[2], (refs[3:5], refs[5:7]), refs[7:]
    right_ref, offset_ref = refs[-2:]
    width = low_ref.shape[1]
    factor = LOG2E / epsilon
    for k, of in enumerate(group):
        at = slice(k * piece, (k + 1) * piece)
        t = block_refs[k][sources[k] : sources[k] + piece, :]
        low_ref[at, :] = t.astype(jnp.bfloat16)
        tt = t.T
        high = tt.astype(jnp.bfloat16)
        low = (tt - high.astype(jnp.float32)).astype(jnp.bfloat16)
        right_ref[0:width, at] = high
        right_ref[width : 2 * width, at] = low
        right_ref[2 * width : 3 * width, at] = high
        squares = jnp.sum(tt * tt, axis=0, keepdims=True)
        potential = potential_of(pot_ref, base, of, piece)
        offset_ref[0:1, at] = potential * factor - squares * (factor / width)
    for side in range(2):
        score_rows(left_refs[side], right_ref, offset_ref, old[side], score_refs[side], *state_refs[side], 256)
        if last:
            top_ref, total_ref = state_refs[side]
            for k in range(top_ref.shape[0] // 128):
                at = slice(k * 128, (k + 1) * 128)
                top = top_ref[at, :].T
                total = total_ref[at, :].T
                highest = jnp.max(top, axis=0, keepdims=True)
                whole = jnp.sum(total * jnp.exp2(top - highest), axis=0, keepdims=True)
                refs[0][side, k : k + 1, :] = highest + jnp.log2(whole)


def log_sum(parts):
    highest = functools.reduce(jnp.maximum, parts)
    return highest + jnp.log2(sum(jnp.exp2(part - highest) for part in parts))


def column_kernel(groups, log_targets, width, *refs):
    count = len(groups)
    score_refs = (refs[:count], refs[count : 2 * count])
    rows_ref, square_ref, column_ref, own_ref = refs[2 * count : 2 * count + 4]
    add_refs = refs[2 * count + 4 :]
    half = lax.axis_index("c")
    group = rows_ref.shape[0] // 2
    mine = lax.axis_index("y") * lax.axis_size("zh") + lax.axis_index("zh")
    for side in range(2):
        parts = [rows_ref[half * group + k, side] for k in range(group)]
        parts += [rows_ref[(1 - half) * group + k, 1 - side] for k in range(group)]
        add = log_targets - log_sum(parts)
        for k in range(add.shape[0]):
            add_refs[side][k * 128 : (k + 1) * 128, :] = jnp.broadcast_to(add[k : k + 1, :], (128, 128)).T
        if side == 0:
            chosen = jnp.where(lax.broadcasted_iota(jnp.int32, add.shape, 0) == mine, add, 0.0)
            chosen = jnp.sum(chosen, axis=0, keepdims=True)
            own_ref[...] = square_ref[...] / width + chosen * (epsilon / LOG2E)
    rows = add_refs[0].shape[0]
    step = 64
    columns = score_refs[0][0].shape[1]
    tiles = [(g, slice(c, c + 128)) for g in range(count) for c in range(0, columns, 128)]

    def sweep(side):
        def one(n, sums):
            at = pl.ds(pl.multiple_of(n * step, step), step)
            add = add_refs[side][at, :]
            out = []
            for (g, c), total in zip(tiles, sums, strict=True):
                v = jnp.exp2(score_refs[side][g][at, c] + add)
                out.append(total + jnp.sum(v.reshape(step // 8, 8, 128), axis=0))
            return tuple(out)

        return one

    sums = tuple(jnp.zeros((8, 128), jnp.float32) for _ in tiles)
    for side in range(2):
        sums = lax.fori_loop(0, rows // step, sweep(side), sums)
    sums = [jnp.sum(total, axis=0, keepdims=True) for total in sums]
    least = jnp.min(functools.reduce(jnp.minimum, sums))
    for g, group in enumerate(groups):
        for k, of in enumerate(group):
            n = (g * len(group) + k) * (columns // 128 // len(group))
            some = sums[n : n + columns // 128 // len(group)]
            column_ref[pl.ds(column_of(of), 1), :] = jnp.log2(jnp.concatenate(some, axis=1))

    @pl.when(jnp.logical_not(least > 2.0**-80))
    def _():
        safe_columns(groups, score_refs, add_refs, column_ref)


def safe_columns(groups, score_refs, add_refs, column_ref):
    rows = add_refs[0].shape[0]
    step = 64
    for g, of in enumerate(groups):
        piece = score_refs[0][g].shape[1] // 2
        for k in range(2):
            at = [slice(c, c + 128) for c in range(k * piece, (k + 1) * piece, 128)]
            tops = [None] * len(at)
            for side in range(2):
                for r in range(0, rows, step):
                    add = add_refs[side][r : r + step, :]
                    for n, c in enumerate(at):
                        v = score_refs[side][g][r : r + step, c] + add
                        v = jnp.max(v.reshape(step // 8, 8, 128), axis=0)
                        tops[n] = v if tops[n] is None else jnp.maximum(tops[n], v)
            tops = [jnp.max(top, axis=0, keepdims=True) for top in tops]
            totals = [None] * len(at)
            for side in range(2):
                for r in range(0, rows, step):
                    add = add_refs[side][r : r + step, :]
                    for n, c in enumerate(at):
                        v = jnp.exp2(score_refs[side][g][r : r + step, c] + add - tops[n])
                        v = jnp.sum(v.reshape(step // 8, 8, 128), axis=0)
                        totals[n] = v if totals[n] is None else totals[n] + v
            outs = [top + jnp.log2(jnp.sum(total, axis=0, keepdims=True)) for top, total in zip(tops, totals, strict=True)]
            column_ref[pl.ds(column_of(of[k]), 1), :] = jnp.concatenate(outs, axis=1)


def map_kernel(groups, block, log_sources, *refs):
    count = len(groups)
    score_refs, refs = refs[:count], refs[count:]
    low_refs, refs = refs[:count], refs[count:]
    add_ref, parts_ref, refs = refs[0], refs[1], refs[2:]
    if log_sources is not None:
        pot_ref, out_ref, own_ref, level_ref, sum_ref = refs
    else:
        out_ref, level_ref, sum_ref = refs
    parts = [parts_ref[k] for k in range(parts_ref.shape[0])]
    level_ref[...] = log_sum(parts)
    if log_sources is not None:
        own = level_ref[pl.ds(column_of((0, False)), 1), :]
        own_ref[...] = potential_of(pot_ref, 0, (0, False), own.shape[1]) - epsilon * (own / LOG2E - log_sources)
    rows = add_ref.shape[0]
    for g, group in enumerate(groups):
        level = jnp.concatenate([level_ref[pl.ds(column_of(of), 1), :] for of in group], axis=1)
        columns = level.shape[1]
        for start in range(0, rows, block):
            at = slice(start, start + block)
            add = add_ref[at, :]
            total = None
            weights = []
            for c in range(0, columns, 128):
                w = jnp.exp2(score_refs[g][at, c : c + 128] + add - level[:, c : c + 128])
                total = w if total is None else total + w
                weights.append(w.astype(jnp.bfloat16))
            part = jnp.dot(
                jnp.concatenate(weights, axis=1), low_refs[g][...], preferred_element_type=jnp.float32
            )
            for r in range(0, block, 128):
                k = (start + r) // 128
                if g == 0:
                    out_ref[k, 0:128, :] = part[r : r + 128, :]
                else:
                    out_ref[k, 0:128, :] += part[r : r + 128, :]
            if g == 0:
                sum_ref[at, :] = total
            else:
                sum_ref[at, :] += total
    for k in range(rows // 128):
        total = jnp.sum(sum_ref[k * 128 : (k + 1) * 128, :].T, axis=0, keepdims=True)
        out_ref[k, 128:136, :] = jnp.broadcast_to(
            jnp.concatenate([total] * (out_ref.shape[2] // 128), axis=1), (8, out_ref.shape[2])
        )


def quotient_kernel(parts_ref, source_ref, target_ref, own_source_ref, own_target_ref, out_ref):
    own_source_ref[...] = source_ref[0, :]
    own_target_ref[...] = target_ref[0, :]
    rows, width = out_ref.shape
    numerator = parts_ref[0, 0:rows, :]
    denominator = parts_ref[0, rows : rows + 8, 0:128]
    for k in range(1, parts_ref.shape[0]):
        numerator = numerator + parts_ref[k, 0:rows, :]
        denominator = denominator + parts_ref[k, rows : rows + 8, 0:128]
    inverse = jnp.broadcast_to(1.0 / denominator[0:1, :], (128, 128)).T
    for c in range(0, width, 128):
        out_ref[:, c : c + 128] = numerator[:, c : c + 128] * inverse


def call(kernel, name, outs, *args, scratch=(), aliases=None):
    return pl.pallas_call(
        kernel,
        out_shape=outs,
        in_specs=[spec()] * len(args),
        out_specs=[spec()] * len(outs),
        scratch_shapes=list(scratch),
        input_output_aliases=aliases or {},
        compiler_params=params(),
        name=name,
    )(*args)


def shards(source_points, target_points, target_potential):
    sizes = {name: lax.axis_size(name) for name in ("x", "zl", "c", "y", "zh")}
    across_x = sizes["x"]
    rows, width = source_points.shape
    piece = target_points.shape[0]
    tgts = sizes["y"] * sizes["zh"]
    sources = sizes["x"] * sizes["zl"] * sizes["c"]
    log_targets = math.log2(target_potential.shape[0] * tgts)
    f32, bf16 = jnp.float32, jnp.bfloat16
    share = rows // tgts

    trade = []
    for zl in range(2):
        for c in range(2):
            for zh in range(2):
                trade.append((zl * 4 + c * 2 + zh, (1 - zl) * 4 + c * 2 + (zh ^ c)))

    def traded(value):
        return lax.ppermute(value, ("zl", "c", "zh"), trade)

    def along(value, by):
        return lax.ppermute(value, "x", [(i, (i + by) % across_x) for i in range(across_x)])

    def twin(value):
        return lax.ppermute(value, "c", [(0, 1), (1, 0)])

    other_points = twin(source_points)
    pot = target_potential.reshape(-1, 128)
    behind = along(target_points, 1)
    ahead = along(target_points, across_x - 1)
    far = along(target_points, 2)
    parcel = [VMEM((2 * piece + pot.shape[0], width), f32)]
    (parcel_start,) = call(functools.partial(pack_kernel, (0, 2 * piece)), "pack", parcel, target_points, pot)
    points = source_points
    (near,) = call(
        functools.partial(pack_kernel, (piece,)), "pack", parcel, parcel_start, behind, aliases={0: 0}
    )
    near = traded(near)
    groups = [
        [(0, False), (3, False)],
        [(1, False), (2, False)],
        [(0, True), (3, True)],
        [(1, True), (2, True)],
    ]
    blocks = [[target_points, behind], [ahead, far], [near, near], None]
    starts = [(0, 0), (0, 0), (0, piece), (0, piece)]
    pots = [(pot, 0), (pot, 0), (near, 2 * piece), (near, 2 * piece)]
    scale = 2.0 * LOG2E / (epsilon * width)
    left, squares = call(
        functools.partial(split_kernel, scale, True),
        "split",
        [VMEM((rows, 3 * width), bf16), VMEM((1, share), f32)],
        points,
    )
    (other_left,) = call(
        functools.partial(split_kernel, scale, False), "split", [VMEM((rows, 3 * width), bf16)], other_points
    )
    own_scores, other_scores, lows, state = [], [], [], ()
    for g, group in enumerate(groups):
        first, last = g == 0, g == len(groups) - 1
        outs = [VMEM((rows, 2 * piece), f32)] * 2 + [VMEM((2 * piece, width), bf16)] + [VMEM((rows, 128), f32)] * 4
        if last:
            outs.append(VMEM((2, rows // 128, 128), f32))
        result = call(
            functools.partial(score_kernel, group, piece, starts[g], pots[g][1], first, last),
            "score",
            outs,
            left,
            other_left,
            *blocks[g],
            pots[g][0],
            *state,
            scratch=[VMEM((3 * width, 2 * piece), bf16), VMEM((8, 2 * piece), f32)],
            aliases={} if first else {3 + len(blocks[g]) + k: 3 + k for k in range(4)},
        )
        own_scores.append(result[0])
        other_scores.append(result[1])
        lows.append(result[2])
        state = tuple(result[3:7])
        if g == 0:
            ahead, far, *state = lax.optimization_barrier((ahead, far) + state)
            blocks[1] = [ahead, far]
            (rest,) = call(
                functools.partial(pack_kernel, (0, piece)), "pack", [VMEM((2 * piece, width), f32)], ahead, far
            )
            rest = traded(rest)
            blocks[3] = [rest, rest]
    levels = result[7]
    row_axes = ("c", "y", "zh")
    spread = jnp.broadcast_to(levels[None], (2 * tgts,) + levels.shape)
    row_levels = lax.all_to_all(spread, row_axes, 0, 0)
    column_level, own_source, add, other_add = call(
        functools.partial(column_kernel, groups, log_targets, width),
        "columns",
        [VMEM((2 * across_x, piece), f32), VMEM((1, share), f32), VMEM((rows, 128), f32), VMEM((rows, 128), f32)],
        *own_scores,
        *other_scores,
        row_levels,
        squares,
    )
    spread = jnp.broadcast_to(column_level[None], (2 * across_x,) + column_level.shape)
    members = []
    for layer in range(2):
        for c in range(2):
            members.append([((k * 2 + zl) * 2 + c) * 2 + (layer ^ (zl & c)) for k in range(across_x) for zl in range(2)])
    column_levels = lax.all_to_all(spread, ("x", "zl", "c", "zh"), 0, 0, axis_index_groups=members)
    scratch = [VMEM(column_level.shape, f32), VMEM((rows, 128), f32)]
    partial_out = VMEM((tgts, share + 8, width), f32)
    (other_map,) = call(
        functools.partial(map_kernel, groups, 256, None),
        "map_other",
        [partial_out],
        *other_scores,
        *lows,
        other_add,
        column_levels,
        scratch=scratch,
    )
    returned = twin(other_map)
    own_map, own_target = call(
        functools.partial(map_kernel, groups, 256, math.log(rows * sources)),
        "map",
        [partial_out, VMEM((1, piece), f32)],
        *own_scores,
        *lows,
        add,
        column_levels,
        pot,
        scratch=scratch,
    )
    summed = own_map + returned
    received = lax.all_to_all(summed, ("y", "zh"), 0, 0)
    results = [jax.ShapeDtypeStruct(dims, f32) for dims in ((share,), (piece,), (share, width))]
    return tuple(call(quotient_kernel, "quotient", results, received, own_source, own_target))


def solution(mesh):
    fine = Mesh(mesh.devices.reshape(4, 2, 2, 4, 2), ("x", "zl", "c", "y", "zh"))
    src, tgt = ("x", "zl", "c"), ("y", "zh")
    return jax.shard_map(
        shards,
        mesh=fine,
        in_specs=(P(src, None), P(tgt + src, None), P(tgt)),
        out_specs=(P(src + tgt), P(tgt + src), P(src + tgt, None)),
        check_vma=False,
    )
```

```python
import functools
import math

import jax
import jax.numpy as jnp
from jax import lax
from jax.experimental import pallas as pl
from jax.experimental.pallas import tpu as pltpu
from jax.sharding import Mesh
from jax.sharding import PartitionSpec as P

epsilon = 0.05
LOG2E = math.log2(math.e)
VMEM = pltpu.VMEM
LIMIT = 18 * 1024 * 1024


def spec():
    return pl.BlockSpec(memory_space=VMEM)


def params():
    return pltpu.CompilerParams(vmem_limit_bytes=LIMIT)


def split_kernel(scale, own, x_ref, out_ref, *square_ref):
    x = x_ref[...]
    width = x.shape[1]
    if own:
        mine = lax.axis_index("y") * lax.axis_size("zh") + lax.axis_index("zh")
        some = x_ref[pl.ds(pl.multiple_of(mine * 128, 128), 128), :]
        square_ref[0][...] = jnp.sum((some * some).T, axis=0, keepdims=True)
    x = x * scale
    high = x.astype(jnp.bfloat16)
    low = (x - high.astype(jnp.float32)).astype(jnp.bfloat16)
    out_ref[:, 0:width] = high
    out_ref[:, width : 2 * width] = high
    out_ref[:, 2 * width : 3 * width] = low


def place(of):
    return lax.rem(lax.axis_index("x") + of[0], lax.axis_size("x"))


def half_of(of):
    half = lax.axis_index("zl")
    return 1 - half if of[1] else half


def piece_of(of):
    return (place(of) * 2 + half_of(of)) * 2 + lax.axis_index("c")


def column_of(of):
    return place(of) * 2 + half_of(of)


def potential_of(pot_ref, base, of, piece):
    lines = piece // 128
    start = base + piece_of(of) * lines
    return jnp.concatenate([pot_ref[pl.ds(start + k, 1), :][:, 0:128] for k in range(lines)], axis=1)


def pack_kernel(starts, *refs):
    out_ref = refs[-1]
    for start, ref in zip(starts, refs[-1 - len(starts) : -1], strict=True):
        rows, width = ref.shape
        out_ref[start : start + rows, 0:width] = ref[...]
        if width < out_ref.shape[1]:
            out_ref[start : start + rows, width:] = jnp.zeros((rows, out_ref.shape[1] - width), jnp.float32)


def score_rows(x_ref, right_ref, offset_ref, old, score_ref, top_ref, total_ref, block):
    rows, columns = score_ref.shape
    for start in range(0, rows, block):
        at = slice(start, start + block)
        score = jnp.dot(x_ref[at, :], right_ref[...], preferred_element_type=jnp.float32)
        score = score + offset_ref[0:1, :]
        score_ref[at, :] = score
        tiles = [score[:, k : k + 128] for k in range(0, columns, 128)]
        top = functools.reduce(jnp.maximum, tiles)
        if old is not None:
            before = old[0][at, :]
            top = jnp.maximum(top, before)
        total = sum(jnp.exp2(tile - top) for tile in tiles)
        if old is not None:
            total = total + old[1][at, :] * jnp.exp2(before - top)
        top_ref[at, :] = top
        total_ref[at, :] = total


def score_kernel(group, piece, sources, base, first, last, *refs):
    left_refs, refs = refs[:2], refs[2:]
    block_refs, pot_ref, refs = refs[: len(sources)], refs[len(sources)], refs[len(sources) + 1 :]
    old = (None, None)
    if not first:
        old, refs = (refs[0:2], refs[2:4]), refs[4:]
    score_refs, low_ref, state_refs, refs = refs[:2], refs[2], (refs[3:5], refs[5:7]), refs[7:]
    right_ref, offset_ref = refs[-2:]
    width = low_ref.shape[1]
    factor = LOG2E / epsilon
    for k, of in enumerate(group):
        at = slice(k * piece, (k + 1) * piece)
        t = block_refs[k][sources[k] : sources[k] + piece, :]
        low_ref[at, :] = t.astype(jnp.bfloat16)
        tt = t.T
        high = tt.astype(jnp.bfloat16)
        low = (tt - high.astype(jnp.float32)).astype(jnp.bfloat16)
        right_ref[0:width, at] = high
        right_ref[width : 2 * width, at] = low
        right_ref[2 * width : 3 * width, at] = high
        squares = jnp.sum(tt * tt, axis=0, keepdims=True)
        potential = potential_of(pot_ref, base, of, piece)
        offset_ref[0:1, at] = potential * factor - squares * (factor / width)
    for side in range(2):
        score_rows(left_refs[side], right_ref, offset_ref, old[side], score_refs[side], *state_refs[side], 256)
        if last:
            top_ref, total_ref = state_refs[side]
            for k in range(top_ref.shape[0] // 128):
                at = slice(k * 128, (k + 1) * 128)
                top = top_ref[at, :].T
                total = total_ref[at, :].T
                highest = jnp.max(top, axis=0, keepdims=True)
                whole = jnp.sum(total * jnp.exp2(top - highest), axis=0, keepdims=True)
                refs[0][side, k : k + 1, :] = highest + jnp.log2(whole)


def log_sum(parts):
    highest = functools.reduce(jnp.maximum, parts)
    return highest + jnp.log2(sum(jnp.exp2(part - highest) for part in parts))


def column_kernel(groups, log_targets, width, *refs):
    count = len(groups)
    score_refs = (refs[:count], refs[count : 2 * count])
    rows_ref, square_ref, column_ref, own_ref = refs[2 * count : 2 * count + 4]
    add_refs = refs[2 * count + 4 :]
    half = lax.axis_index("c")
    group = rows_ref.shape[0] // 2
    mine = lax.axis_index("y") * lax.axis_size("zh") + lax.axis_index("zh")
    for side in range(2):
        parts = [rows_ref[half * group + k, side] for k in range(group)]
        parts += [rows_ref[(1 - half) * group + k, 1 - side] for k in range(group)]
        add = log_targets - log_sum(parts)
        for k in range(add.shape[0]):
            add_refs[side][k * 128 : (k + 1) * 128, :] = jnp.broadcast_to(add[k : k + 1, :], (128, 128)).T
        if side == 0:
            chosen = jnp.where(lax.broadcasted_iota(jnp.int32, add.shape, 0) == mine, add, 0.0)
            chosen = jnp.sum(chosen, axis=0, keepdims=True)
            own_ref[...] = square_ref[...] / width + chosen * (epsilon / LOG2E)
    rows = add_refs[0].shape[0]
    step = 64
    columns = score_refs[0][0].shape[1]
    tiles = [(g, slice(c, c + 128)) for g in range(count) for c in range(0, columns, 128)]

    def sweep(side):
        def one(n, sums):
            at = pl.ds(pl.multiple_of(n * step, step), step)
            add = add_refs[side][at, :]
            out = []
            for (g, c), total in zip(tiles, sums, strict=True):
                v = jnp.exp2(score_refs[side][g][at, c] + add)
                out.append(total + jnp.sum(v.reshape(step // 8, 8, 128), axis=0))
            return tuple(out)

        return one

    sums = tuple(jnp.zeros((8, 128), jnp.float32) for _ in tiles)
    for side in range(2):
        sums = lax.fori_loop(0, rows // step, sweep(side), sums)
    sums = [jnp.sum(total, axis=0, keepdims=True) for total in sums]
    least = jnp.min(functools.reduce(jnp.minimum, sums))
    for g, group in enumerate(groups):
        for k, of in enumerate(group):
            n = (g * len(group) + k) * (columns // 128 // len(group))
            some = sums[n : n + columns // 128 // len(group)]
            column_ref[pl.ds(column_of(of), 1), :] = jnp.log2(jnp.concatenate(some, axis=1))

    @pl.when(jnp.logical_not(least > 2.0**-80))
    def _():
        safe_columns(groups, score_refs, add_refs, column_ref)


def safe_columns(groups, score_refs, add_refs, column_ref):
    rows = add_refs[0].shape[0]
    step = 64
    for g, of in enumerate(groups):
        piece = score_refs[0][g].shape[1] // 2
        for k in range(2):
            at = [slice(c, c + 128) for c in range(k * piece, (k + 1) * piece, 128)]
            tops = [None] * len(at)
            for side in range(2):
                for r in range(0, rows, step):
                    add = add_refs[side][r : r + step, :]
                    for n, c in enumerate(at):
                        v = score_refs[side][g][r : r + step, c] + add
                        v = jnp.max(v.reshape(step // 8, 8, 128), axis=0)
                        tops[n] = v if tops[n] is None else jnp.maximum(tops[n], v)
            tops = [jnp.max(top, axis=0, keepdims=True) for top in tops]
            totals = [None] * len(at)
            for side in range(2):
                for r in range(0, rows, step):
                    add = add_refs[side][r : r + step, :]
                    for n, c in enumerate(at):
                        v = jnp.exp2(score_refs[side][g][r : r + step, c] + add - tops[n])
                        v = jnp.sum(v.reshape(step // 8, 8, 128), axis=0)
                        totals[n] = v if totals[n] is None else totals[n] + v
            outs = [top + jnp.log2(jnp.sum(total, axis=0, keepdims=True)) for top, total in zip(tops, totals, strict=True)]
            column_ref[pl.ds(column_of(of[k]), 1), :] = jnp.concatenate(outs, axis=1)


def map_kernel(groups, block, log_sources, *refs):
    count = len(groups)
    score_refs, refs = refs[:count], refs[count:]
    low_refs, refs = refs[:count], refs[count:]
    add_ref, parts_ref, refs = refs[0], refs[1], refs[2:]
    if log_sources is not None:
        pot_ref, out_ref, own_ref, level_ref = refs
    else:
        out_ref, level_ref = refs
    parts = [parts_ref[k] for k in range(parts_ref.shape[0])]
    level_ref[...] = log_sum(parts)
    if log_sources is not None:
        own = level_ref[pl.ds(column_of((0, False)), 1), :]
        own_ref[...] = potential_of(pot_ref, 0, (0, False), own.shape[1]) - epsilon * (own / LOG2E - log_sources)
    rows = add_ref.shape[0]
    levels = [
        jnp.concatenate([level_ref[pl.ds(column_of(of), 1), :] for of in group], axis=1) for group in groups
    ]
    for start in range(0, rows, block):
        at = slice(start, start + block)
        add = add_ref[at, :]
        total = None
        result = None
        for g, level in enumerate(levels):
            weights = []
            for c in range(0, level.shape[1], 128):
                w = jnp.exp2(score_refs[g][at, c : c + 128] + add - level[:, c : c + 128]).astype(jnp.bfloat16)
                total = w.astype(jnp.float32) if total is None else total + w.astype(jnp.float32)
                weights.append(w)
            part = jnp.dot(
                jnp.concatenate(weights, axis=1), low_refs[g][...], preferred_element_type=jnp.float32
            )
            result = part if result is None else result + part
        for r in range(0, block, 128):
            k = (start + r) // 128
            out_ref[k, 0:128, :] = result[r : r + 128, :]
            sums = jnp.sum(total[r : r + 128, :].T, axis=0, keepdims=True)
            out_ref[k, 128:136, :] = jnp.broadcast_to(
                jnp.concatenate([sums] * (out_ref.shape[2] // 128), axis=1), (8, out_ref.shape[2])
            )


def quotient_kernel(parts_ref, source_ref, target_ref, own_source_ref, own_target_ref, out_ref):
    own_source_ref[...] = source_ref[0, :]
    own_target_ref[...] = target_ref[0, :]
    rows, width = out_ref.shape
    numerator = parts_ref[0, 0:rows, :]
    denominator = parts_ref[0, rows : rows + 8, 0:128]
    for k in range(1, parts_ref.shape[0]):
        numerator = numerator + parts_ref[k, 0:rows, :]
        denominator = denominator + parts_ref[k, rows : rows + 8, 0:128]
    inverse = jnp.broadcast_to(1.0 / denominator[0:1, :], (128, 128)).T
    for c in range(0, width, 128):
        out_ref[:, c : c + 128] = numerator[:, c : c + 128] * inverse


def call(kernel, name, outs, *args, scratch=(), aliases=None):
    return pl.pallas_call(
        kernel,
        out_shape=outs,
        in_specs=[spec()] * len(args),
        out_specs=[spec()] * len(outs),
        scratch_shapes=list(scratch),
        input_output_aliases=aliases or {},
        compiler_params=params(),
        name=name,
    )(*args)


def shards(source_points, target_points, target_potential):
    sizes = {name: lax.axis_size(name) for name in ("x", "zl", "c", "y", "zh")}
    across_x = sizes["x"]
    rows, width = source_points.shape
    piece = target_points.shape[0]
    tgts = sizes["y"] * sizes["zh"]
    sources = sizes["x"] * sizes["zl"] * sizes["c"]
    log_targets = math.log2(target_potential.shape[0] * tgts)
    f32, bf16 = jnp.float32, jnp.bfloat16
    share = rows // tgts

    trade = []
    for zl in range(2):
        for c in range(2):
            for zh in range(2):
                trade.append((zl * 4 + c * 2 + zh, (1 - zl) * 4 + c * 2 + (zh ^ c)))

    def traded(value):
        return lax.ppermute(value, ("zl", "c", "zh"), trade)

    def along(value, by):
        return lax.ppermute(value, "x", [(i, (i + by) % across_x) for i in range(across_x)])

    def twin(value):
        return lax.ppermute(value, "c", [(0, 1), (1, 0)])

    other_points = twin(source_points)
    pot = target_potential.reshape(-1, 128)
    far = along(target_points, 2)
    behind = along(target_points, 1)
    ahead = along(target_points, across_x - 1)
    parcel = [VMEM((2 * piece + pot.shape[0], width), f32)]
    (parcel_start,) = call(functools.partial(pack_kernel, (0, 2 * piece)), "pack", parcel, target_points, pot)
    points = source_points
    (near,) = call(
        functools.partial(pack_kernel, (piece,)), "pack", parcel, parcel_start, behind, aliases={0: 0}
    )
    near = traded(near)
    groups = [
        [(0, False), (3, False)],
        [(1, False), (2, False)],
        [(0, True), (3, True)],
        [(1, True), (2, True)],
    ]
    blocks = [[target_points, behind], [ahead, far], [near, near], None]
    starts = [(0, 0), (0, 0), (0, piece), (0, piece)]
    pots = [(pot, 0), (pot, 0), (near, 2 * piece), (near, 2 * piece)]
    scale = 2.0 * LOG2E / (epsilon * width)
    left, squares = call(
        functools.partial(split_kernel, scale, True),
        "split",
        [VMEM((rows, 3 * width), bf16), VMEM((1, share), f32)],
        points,
    )
    (other_left,) = call(
        functools.partial(split_kernel, scale, False), "split", [VMEM((rows, 3 * width), bf16)], other_points
    )
    own_scores, other_scores, lows, state = [], [], [], ()
    for g, group in enumerate(groups):
        first, last = g == 0, g == len(groups) - 1
        outs = [VMEM((rows, 2 * piece), f32)] * 2 + [VMEM((2 * piece, width), bf16)] + [VMEM((rows, 128), f32)] * 4
        if last:
            outs.append(VMEM((2, rows // 128, 128), f32))
        result = call(
            functools.partial(score_kernel, group, piece, starts[g], pots[g][1], first, last),
            "score",
            outs,
            left,
            other_left,
            *blocks[g],
            pots[g][0],
            *state,
            scratch=[VMEM((3 * width, 2 * piece), bf16), VMEM((8, 2 * piece), f32)],
            aliases={} if first else {3 + len(blocks[g]) + k: 3 + k for k in range(4)},
        )
        own_scores.append(result[0])
        other_scores.append(result[1])
        lows.append(result[2])
        state = tuple(result[3:7])
        if g == 0:
            ahead, far, squares = lax.optimization_barrier((ahead, far, squares))
            blocks[1] = [ahead, far]
            (rest,) = call(
                functools.partial(pack_kernel, (0, piece)), "pack", [VMEM((2 * piece, width), f32)], ahead, far
            )
            rest = traded(rest)
            blocks[3] = [rest, rest]
    levels = result[7]
    row_axes = ("c", "y", "zh")
    spread = jnp.broadcast_to(levels[None], (2 * tgts,) + levels.shape)
    row_levels = lax.all_to_all(spread, row_axes, 0, 0)
    column_level, own_source, add, other_add = call(
        functools.partial(column_kernel, groups, log_targets, width),
        "columns",
        [VMEM((2 * across_x, piece), f32), VMEM((1, share), f32), VMEM((rows, 128), f32), VMEM((rows, 128), f32)],
        *own_scores,
        *other_scores,
        row_levels,
        squares,
    )
    spread = jnp.broadcast_to(column_level[None], (2 * across_x,) + column_level.shape)
    members = []
    for layer in range(2):
        for c in range(2):
            members.append([((k * 2 + zl) * 2 + c) * 2 + (layer ^ (zl & c)) for k in range(across_x) for zl in range(2)])
    column_levels = lax.all_to_all(spread, ("x", "zl", "c", "zh"), 0, 0, axis_index_groups=members)
    scratch = [VMEM(column_level.shape, f32)]
    partial_out = VMEM((tgts, share + 8, width), f32)
    (other_map,) = call(
        functools.partial(map_kernel, groups, 512, None),
        "map_other",
        [partial_out],
        *other_scores,
        *lows,
        other_add,
        column_levels,
        scratch=scratch,
    )
    returned = twin(other_map)
    own_map, own_target = call(
        functools.partial(map_kernel, groups, 512, math.log(rows * sources)),
        "map",
        [partial_out, VMEM((1, piece), f32)],
        *own_scores,
        *lows,
        add,
        column_levels,
        pot,
        scratch=scratch,
    )
    summed = own_map + returned
    received = lax.all_to_all(summed, ("y", "zh"), 0, 0)
    results = [jax.ShapeDtypeStruct(dims, f32) for dims in ((share,), (piece,), (share, width))]
    return tuple(call(quotient_kernel, "quotient", results, received, own_source, own_target))


def solution(mesh):
    fine = Mesh(mesh.devices.reshape(4, 2, 2, 4, 2), ("x", "zl", "c", "y", "zh"))
    src, tgt = ("x", "zl", "c"), ("y", "zh")
    return jax.shard_map(
        shards,
        mesh=fine,
        in_specs=(P(src, None), P(tgt + src, None), P(tgt)),
        out_specs=(P(src + tgt), P(tgt + src), P(src + tgt, None)),
        check_vma=False,
    )
```

```python
import functools
import math

import jax
import jax.numpy as jnp
from jax import lax
from jax.experimental import pallas as pl
from jax.experimental.pallas import tpu as pltpu
from jax.sharding import Mesh
from jax.sharding import PartitionSpec as P

epsilon = 0.05
LOG2E = math.log2(math.e)
VMEM = pltpu.VMEM
LIMIT = 18 * 1024 * 1024


def spec():
    return pl.BlockSpec(memory_space=VMEM)


def params():
    return pltpu.CompilerParams(vmem_limit_bytes=LIMIT)


def split_kernel(scale, own, x_ref, out_ref, *square_ref):
    x = x_ref[...]
    width = x.shape[1]
    if own:
        mine = lax.axis_index("y") * lax.axis_size("zh") + lax.axis_index("zh")
        some = x_ref[pl.ds(pl.multiple_of(mine * 128, 128), 128), :]
        square_ref[0][...] = jnp.sum((some * some).T, axis=0, keepdims=True)
    x = x * scale
    high = x.astype(jnp.bfloat16)
    low = (x - high.astype(jnp.float32)).astype(jnp.bfloat16)
    out_ref[:, 0:width] = high
    out_ref[:, width : 2 * width] = high
    out_ref[:, 2 * width : 3 * width] = low


def place(of):
    return lax.rem(lax.axis_index("x") + of[0], lax.axis_size("x"))


def half_of(of):
    half = lax.axis_index("zl")
    return 1 - half if of[1] else half


def piece_of(of):
    return (place(of) * 2 + half_of(of)) * 2 + lax.axis_index("c")


def column_of(of):
    return place(of) * 2 + half_of(of)


def potential_of(pot_ref, base, of, piece):
    lines = piece // 128
    start = base + piece_of(of) * lines
    return jnp.concatenate([pot_ref[pl.ds(start + k, 1), :][:, 0:128] for k in range(lines)], axis=1)


def pack_kernel(starts, *refs):
    out_ref = refs[-1]
    for start, ref in zip(starts, refs[-1 - len(starts) : -1], strict=True):
        rows, width = ref.shape
        out_ref[start : start + rows, 0:width] = ref[...]
        if width < out_ref.shape[1]:
            out_ref[start : start + rows, width:] = jnp.zeros((rows, out_ref.shape[1] - width), jnp.float32)


def score_rows(x_ref, right_ref, offset_ref, old, score_ref, top_ref, total_ref, block):
    rows, columns = score_ref.shape
    for start in range(0, rows, block):
        at = slice(start, start + block)
        score = jnp.dot(x_ref[at, :], right_ref[...], preferred_element_type=jnp.float32)
        score = score + offset_ref[0:1, :]
        score_ref[at, :] = score
        tiles = [score[:, k : k + 128] for k in range(0, columns, 128)]
        top = functools.reduce(jnp.maximum, tiles)
        if old is not None:
            before = old[0][at, :]
            top = jnp.maximum(top, before)
        total = sum(jnp.exp2(tile - top) for tile in tiles)
        if old is not None:
            total = total + old[1][at, :] * jnp.exp2(before - top)
        top_ref[at, :] = top
        total_ref[at, :] = total


def score_kernel(group, piece, sources, base, first, last, *refs):
    left_refs, refs = refs[:2], refs[2:]
    block_refs, pot_ref, refs = refs[: len(sources)], refs[len(sources)], refs[len(sources) + 1 :]
    old = (None, None)
    if not first:
        old, refs = (refs[0:2], refs[2:4]), refs[4:]
    score_refs, low_ref, state_refs, refs = refs[:2], refs[2], (refs[3:5], refs[5:7]), refs[7:]
    right_ref, offset_ref = refs[-2:]
    width = low_ref.shape[1]
    factor = LOG2E / epsilon
    for k, of in enumerate(group):
        at = slice(k * piece, (k + 1) * piece)
        t = block_refs[k][sources[k] : sources[k] + piece, :]
        low_ref[at, :] = t.astype(jnp.bfloat16)
        tt = t.T
        high = tt.astype(jnp.bfloat16)
        low = (tt - high.astype(jnp.float32)).astype(jnp.bfloat16)
        right_ref[0:width, at] = high
        right_ref[width : 2 * width, at] = low
        right_ref[2 * width : 3 * width, at] = high
        squares = jnp.sum(tt * tt, axis=0, keepdims=True)
        potential = potential_of(pot_ref, base, of, piece)
        offset_ref[0:1, at] = potential * factor - squares * (factor / width)
    for side in range(2):
        score_rows(left_refs[side], right_ref, offset_ref, old[side], score_refs[side], *state_refs[side], 256)
        if last:
            top_ref, total_ref = state_refs[side]
            for k in range(top_ref.shape[0] // 128):
                at = slice(k * 128, (k + 1) * 128)
                top = top_ref[at, :].T
                total = total_ref[at, :].T
                highest = jnp.max(top, axis=0, keepdims=True)
                whole = jnp.sum(total * jnp.exp2(top - highest), axis=0, keepdims=True)
                refs[0][side, k : k + 1, :] = highest + jnp.log2(whole)


def log_sum(parts):
    highest = functools.reduce(jnp.maximum, parts)
    return highest + jnp.log2(sum(jnp.exp2(part - highest) for part in parts))


def column_kernel(groups, log_targets, width, *refs):
    count = len(groups)
    score_refs = (refs[:count], refs[count : 2 * count])
    rows_ref, square_ref, column_ref, own_ref = refs[2 * count : 2 * count + 4]
    add_refs = refs[2 * count + 4 :]
    half = lax.axis_index("c")
    group = rows_ref.shape[0] // 2
    mine = lax.axis_index("y") * lax.axis_size("zh") + lax.axis_index("zh")
    for side in range(2):
        parts = [rows_ref[2 * k + half, side] for k in range(group)]
        parts += [rows_ref[2 * k + 1 - half, 1 - side] for k in range(group)]
        add = log_targets - log_sum(parts)
        for k in range(add.shape[0]):
            add_refs[side][k * 128 : (k + 1) * 128, :] = jnp.broadcast_to(add[k : k + 1, :], (128, 128)).T
        if side == 0:
            chosen = jnp.where(lax.broadcasted_iota(jnp.int32, add.shape, 0) == mine, add, 0.0)
            chosen = jnp.sum(chosen, axis=0, keepdims=True)
            own_ref[...] = square_ref[...] / width + chosen * (epsilon / LOG2E)
    rows = add_refs[0].shape[0]
    step = 64
    columns = score_refs[0][0].shape[1]
    tiles = [(g, slice(c, c + 128)) for g in range(count) for c in range(0, columns, 128)]

    def sweep(side):
        def one(n, sums):
            at = pl.ds(pl.multiple_of(n * step, step), step)
            add = add_refs[side][at, :]
            out = []
            for (g, c), total in zip(tiles, sums, strict=True):
                v = jnp.exp2(score_refs[side][g][at, c] + add)
                out.append(total + jnp.sum(v.reshape(step // 8, 8, 128), axis=0))
            return tuple(out)

        return one

    sums = tuple(jnp.zeros((8, 128), jnp.float32) for _ in tiles)
    for side in range(2):
        sums = lax.fori_loop(0, rows // step, sweep(side), sums)
    sums = [jnp.sum(total, axis=0, keepdims=True) for total in sums]
    least = jnp.min(functools.reduce(jnp.minimum, sums))
    for g, group in enumerate(groups):
        for k, of in enumerate(group):
            n = (g * len(group) + k) * (columns // 128 // len(group))
            some = sums[n : n + columns // 128 // len(group)]
            column_ref[pl.ds(column_of(of), 1), :] = jnp.log2(jnp.concatenate(some, axis=1))

    @pl.when(jnp.logical_not(least > 2.0**-80))
    def _():
        safe_columns(groups, score_refs, add_refs, column_ref)


def safe_columns(groups, score_refs, add_refs, column_ref):
    rows = add_refs[0].shape[0]
    step = 64
    for g, of in enumerate(groups):
        piece = score_refs[0][g].shape[1] // 2
        for k in range(2):
            at = [slice(c, c + 128) for c in range(k * piece, (k + 1) * piece, 128)]
            tops = [None] * len(at)
            for side in range(2):
                for r in range(0, rows, step):
                    add = add_refs[side][r : r + step, :]
                    for n, c in enumerate(at):
                        v = score_refs[side][g][r : r + step, c] + add
                        v = jnp.max(v.reshape(step // 8, 8, 128), axis=0)
                        tops[n] = v if tops[n] is None else jnp.maximum(tops[n], v)
            tops = [jnp.max(top, axis=0, keepdims=True) for top in tops]
            totals = [None] * len(at)
            for side in range(2):
                for r in range(0, rows, step):
                    add = add_refs[side][r : r + step, :]
                    for n, c in enumerate(at):
                        v = jnp.exp2(score_refs[side][g][r : r + step, c] + add - tops[n])
                        v = jnp.sum(v.reshape(step // 8, 8, 128), axis=0)
                        totals[n] = v if totals[n] is None else totals[n] + v
            outs = [top + jnp.log2(jnp.sum(total, axis=0, keepdims=True)) for top, total in zip(tops, totals, strict=True)]
            column_ref[pl.ds(column_of(of[k]), 1), :] = jnp.concatenate(outs, axis=1)


def map_kernel(groups, block, log_sources, *refs):
    count = len(groups)
    score_refs, refs = refs[:count], refs[count:]
    low_refs, refs = refs[:count], refs[count:]
    add_ref, parts_ref, refs = refs[0], refs[1], refs[2:]
    if log_sources is not None:
        pot_ref, out_ref, own_ref, level_ref = refs
    else:
        out_ref, level_ref = refs
    parts = [parts_ref[k] for k in range(parts_ref.shape[0])]
    level_ref[...] = log_sum(parts)
    if log_sources is not None:
        own = level_ref[pl.ds(column_of((0, False)), 1), :]
        own_ref[...] = potential_of(pot_ref, 0, (0, False), own.shape[1]) - epsilon * (own / LOG2E - log_sources)
    rows = add_ref.shape[0]
    levels = [
        jnp.concatenate([level_ref[pl.ds(column_of(of), 1), :] for of in group], axis=1) for group in groups
    ]
    for start in range(0, rows, block):
        at = slice(start, start + block)
        add = add_ref[at, :]
        total = None
        result = None
        for g, level in enumerate(levels):
            weights = []
            for c in range(0, level.shape[1], 128):
                w = jnp.exp2(score_refs[g][at, c : c + 128] + add - level[:, c : c + 128]).astype(jnp.bfloat16)
                total = w.astype(jnp.float32) if total is None else total + w.astype(jnp.float32)
                weights.append(w)
            part = jnp.dot(
                jnp.concatenate(weights, axis=1), low_refs[g][...], preferred_element_type=jnp.float32
            )
            result = part if result is None else result + part
        for r in range(0, block, 128):
            k = (start + r) // 128
            out_ref[k, 0:128, :] = result[r : r + 128, :]
            sums = jnp.sum(total[r : r + 128, :].T, axis=0, keepdims=True)
            out_ref[k, 128:136, :] = jnp.broadcast_to(
                jnp.concatenate([sums] * (out_ref.shape[2] // 128), axis=1), (8, out_ref.shape[2])
            )


def quotient_kernel(parts_ref, source_ref, target_ref, own_source_ref, own_target_ref, out_ref):
    own_source_ref[...] = source_ref[0, :]
    own_target_ref[...] = target_ref[0, :]
    rows, width = out_ref.shape
    numerator = parts_ref[0, 0:rows, :]
    denominator = parts_ref[0, rows : rows + 8, 0:128]
    for k in range(1, parts_ref.shape[0]):
        numerator = numerator + parts_ref[k, 0:rows, :]
        denominator = denominator + parts_ref[k, rows : rows + 8, 0:128]
    inverse = jnp.broadcast_to(1.0 / denominator[0:1, :], (128, 128)).T
    for c in range(0, width, 128):
        out_ref[:, c : c + 128] = numerator[:, c : c + 128] * inverse


def call(kernel, name, outs, *args, scratch=(), aliases=None):
    return pl.pallas_call(
        kernel,
        out_shape=outs,
        in_specs=[spec()] * len(args),
        out_specs=[spec()] * len(outs),
        scratch_shapes=list(scratch),
        input_output_aliases=aliases or {},
        compiler_params=params(),
        name=name,
    )(*args)


def shards(source_points, target_points, target_potential):
    sizes = {name: lax.axis_size(name) for name in ("x", "zl", "c", "y", "zh")}
    across_x = sizes["x"]
    rows, width = source_points.shape
    piece = target_points.shape[0]
    tgts = sizes["y"] * sizes["zh"]
    sources = sizes["x"] * sizes["zl"] * sizes["c"]
    log_targets = math.log2(target_potential.shape[0] * tgts)
    f32, bf16 = jnp.float32, jnp.bfloat16
    share = rows // tgts

    trade = []
    for zl in range(2):
        for c in range(2):
            for zh in range(2):
                trade.append((zl * 4 + c * 2 + zh, (1 - zl) * 4 + c * 2 + (zh ^ c)))

    def traded(value):
        return lax.ppermute(value, ("zl", "c", "zh"), trade)

    def along(value, by):
        return lax.ppermute(value, "x", [(i, (i + by) % across_x) for i in range(across_x)])

    def twin(value):
        return lax.ppermute(value, "c", [(0, 1), (1, 0)])

    other_points = twin(source_points)
    pot = target_potential.reshape(-1, 128)
    far = along(target_points, 2)
    behind = along(target_points, 1)
    ahead = along(target_points, across_x - 1)
    parcel = [VMEM((2 * piece + pot.shape[0], width), f32)]
    (parcel_start,) = call(functools.partial(pack_kernel, (0, 2 * piece)), "pack", parcel, target_points, pot)
    points = source_points
    (near,) = call(
        functools.partial(pack_kernel, (piece,)), "pack", parcel, parcel_start, behind, aliases={0: 0}
    )
    near = traded(near)
    groups = [
        [(0, False), (3, False)],
        [(1, False), (2, False)],
        [(0, True), (3, True)],
        [(1, True), (2, True)],
    ]
    blocks = [[target_points, behind], [ahead, far], [near, near], None]
    starts = [(0, 0), (0, 0), (0, piece), (0, piece)]
    pots = [(pot, 0), (pot, 0), (near, 2 * piece), (near, 2 * piece)]
    scale = 2.0 * LOG2E / (epsilon * width)
    left, squares = call(
        functools.partial(split_kernel, scale, True),
        "split",
        [VMEM((rows, 3 * width), bf16), VMEM((1, share), f32)],
        points,
    )
    (other_left,) = call(
        functools.partial(split_kernel, scale, False), "split", [VMEM((rows, 3 * width), bf16)], other_points
    )
    own_scores, other_scores, lows, state = [], [], [], ()
    for g, group in enumerate(groups):
        first, last = g == 0, g == len(groups) - 1
        outs = [VMEM((rows, 2 * piece), f32)] * 2 + [VMEM((2 * piece, width), bf16)] + [VMEM((rows, 128), f32)] * 4
        if last:
            outs.append(VMEM((2, rows // 128, 128), f32))
        result = call(
            functools.partial(score_kernel, group, piece, starts[g], pots[g][1], first, last),
            "score",
            outs,
            left,
            other_left,
            *blocks[g],
            pots[g][0],
            *state,
            scratch=[VMEM((3 * width, 2 * piece), bf16), VMEM((8, 2 * piece), f32)],
            aliases={} if first else {3 + len(blocks[g]) + k: 3 + k for k in range(4)},
        )
        own_scores.append(result[0])
        other_scores.append(result[1])
        lows.append(result[2])
        state = tuple(result[3:7])
        if g == 0:
            ahead, far, squares = lax.optimization_barrier((ahead, far, squares))
            blocks[1] = [ahead, far]
            (rest,) = call(
                functools.partial(pack_kernel, (0, piece)), "pack", [VMEM((2 * piece, width), f32)], ahead, far
            )
            rest = traded(rest)
            blocks[3] = [rest, rest]
    levels = result[7]
    row_axes = ("y", "zh", "c")
    spread = jnp.broadcast_to(levels[None], (2 * tgts,) + levels.shape)
    row_levels = lax.all_to_all(spread, row_axes, 0, 0)
    column_level, own_source, add, other_add = call(
        functools.partial(column_kernel, groups, log_targets, width),
        "columns",
        [VMEM((2 * across_x, piece), f32), VMEM((1, share), f32), VMEM((rows, 128), f32), VMEM((rows, 128), f32)],
        *own_scores,
        *other_scores,
        row_levels,
        squares,
    )
    spread = jnp.broadcast_to(column_level[None], (2 * across_x,) + column_level.shape)
    members = []
    for layer in range(2):
        for c in range(2):
            members.append([((k * 2 + zl) * 2 + c) * 2 + (layer ^ (zl & c)) for zl in range(2) for k in range(across_x)])
    column_levels = lax.all_to_all(spread, ("x", "zl", "c", "zh"), 0, 0, axis_index_groups=members)
    scratch = [VMEM(column_level.shape, f32)]
    partial_out = VMEM((tgts, share + 8, width), f32)
    (other_map,) = call(
        functools.partial(map_kernel, groups, 512, None),
        "map_other",
        [partial_out],
        *other_scores,
        *lows,
        other_add,
        column_levels,
        scratch=scratch,
    )
    returned = twin(other_map)
    own_map, own_target = call(
        functools.partial(map_kernel, groups, 512, math.log(rows * sources)),
        "map",
        [partial_out, VMEM((1, piece), f32)],
        *own_scores,
        *lows,
        add,
        column_levels,
        pot,
        scratch=scratch,
    )
    summed = own_map + returned
    received = lax.all_to_all(summed, ("y", "zh"), 0, 0)
    results = [jax.ShapeDtypeStruct(dims, f32) for dims in ((share,), (piece,), (share, width))]
    return tuple(call(quotient_kernel, "quotient", results, received, own_source, own_target))


def solution(mesh):
    fine = Mesh(mesh.devices.reshape(4, 2, 2, 4, 2), ("x", "zl", "c", "y", "zh"))
    src, tgt = ("x", "zl", "c"), ("y", "zh")
    return jax.shard_map(
        shards,
        mesh=fine,
        in_specs=(P(src, None), P(tgt + src, None), P(tgt)),
        out_specs=(P(src + tgt), P(tgt + src), P(src + tgt, None)),
        check_vma=False,
    )
```
